512 devices in a mesh: tile: 16 (over y, core), slab: 32 (over z, x).
Axes of the slice: x: 4, y: 8, z: 8, core: 2. Of those that a mesh axis runs over, the one named last changes fastest.
Arguments:
- field: float32 [512, 1024, 512], P('slab', 'tile'), may hold values from -6 to 6
- arc_ids: int32 [512, 1024, 512], P('slab', 'tile'), may hold values from 0 to 63
- arc_tf: int32 [64], replicated, may hold values from 0 to 15
- tf_table: bfloat16 [6, 16], replicated, may hold values from -2 to 12, as said below
Outputs:
- frame: float32 [4, 1024, 512], P(None, 'tile')
The draws below stay inside these ranges and needn't reach their ends.
Inputs may be any that keep to these rules, and one draw needn't show every extreme that they name: `tf_table`: rows 0 to 2 are colours in 0 to 1, row 3 an extinction in 0.3 to 12, row 4 a centre value in -2 to 2, row 5 an inverse width in 0.4 to 1.5.
All inputs are finite; a program needn't handle non-finite values.
Results may differ from the reference program's by a relative error of at most 0.0003.
Values sent between devices are 32-bit elements; how exact they have to be, the bound alone decides.
No kernel may reach another device: no remote copies, remote signals or barrier semaphores. Data moves between devices by JAX's collectives and lax.ppermute only.
A program may use at most 128 MiB of HBM per device.

```python
import math
import jax
import jax.numpy as jnp
from jax import lax

NX = 512
ARCS = 64
TFN = 16
NY = 1024
NZ = 512


def draw_tf_table(key, part):
    key = jax.random.fold_in(key, 17)
    key_colour, key_ext, key_centre, key_width = jax.random.split(key, 4)
    colour = jax.random.uniform(key_colour, (3, TFN), jnp.float32, 0.1, 1.0)
    centre = jax.random.uniform(key_centre, (1, TFN), jnp.float32, -1.5, 1.5)
    extinction = jnp.exp(jax.random.uniform(key_ext, (1, TFN), jnp.float32, math.log(0.3), math.log(12.0)))
    widths = jax.random.uniform(key_width, (1, TFN), jnp.float32, 0.4, 1.5)
    return jnp.concatenate([colour, extinction, centre, widths], axis=0).astype(jnp.bfloat16)


def set_ends(array, key, smallest, largest):
    longest = array.shape.index(max(array.shape))
    spots = []
    for shift in (0, 1):
        where = [jax.random.randint(jax.random.fold_in(key, axis), (), 0, length) for axis, length in enumerate(array.shape)]
        where[longest] = (where[longest] + shift) % array.shape[longest]
        spots.append(tuple(where))
    return array.at[spots[0]].set(smallest).at[spots[1]].set(largest)


def block_scale(stream_key, extent, cuts, smallest, largest):
    def one(dim, shards_of):
        draws = jax.random.uniform(jax.random.fold_in(jax.random.fold_in(stream_key, 6), dim), (shards_of,), jnp.float32, smallest / len(cuts), largest / len(cuts))
        return jnp.repeat(jnp.exp(draws), extent[dim] // shards_of).reshape((-1,) + (1,) * (len(extent) - dim - 1))

    factor_of = one(*cuts[0])
    for cut in cuts[1:]:
        factor_of = factor_of * one(*cut)
    return factor_of


def noise(own_key, shape, deviation, limit, cuts=(), kind=jnp.bfloat16):
    factor_of = block_scale(own_key, shape, cuts, -0.22, 0.18) if cuts else 1.0
    drawn = jax.random.normal(own_key, shape, jnp.float32) * deviation * factor_of
    return jnp.minimum(jnp.maximum(drawn, -limit), limit).astype(kind)


def setup_inputs(seed: int = 0) -> dict:
    key_list = jax.random.split(jax.random.key(seed), 5)
    field = noise(key_list[0], (NZ, NY, NX), 1.0, 6.0, ((0, 32), (1, 16)), jnp.float32)
    arc_ids = set_ends(jax.random.randint(key_list[1], (NZ, NY, NX), 0, ARCS), jax.random.fold_in(key_list[1], 1), 0, ARCS - 1).astype(jnp.int32)
    arc_tf = set_ends(jax.random.randint(key_list[2], (ARCS,), 0, TFN), jax.random.fold_in(key_list[2], 1), 0, TFN - 1).astype(jnp.int32)
    tf_table = draw_tf_table(jax.random.fold_in(key_list[4], 71), 0)
    return dict(field=field, arc_ids=arc_ids, arc_tf=arc_tf, tf_table=tf_table)


def optics(center, slope_across, slope_down, slope_depth, looked, step_len):
    lambert = 0.48 * slope_across + 0.6 * slope_down + 0.64 * slope_depth
    shading = 0.35 + 0.65 * jnp.abs(lambert) / jnp.sqrt(1.0 + slope_across * slope_across + slope_down * slope_down + slope_depth * slope_depth)
    extinction = looked[3] * jnp.exp(-jnp.square(looked[5] * (center - looked[4])))
    passing = jnp.exp(-extinction * step_len)
    weight = (1.0 - passing) * shading
    return (passing, weight[None] * looked[:3])

def reference(field, arc_ids, arc_tf, tf_table):
    arc_params = tf_table[:, arc_tf]
    step_len = 2.0 / NZ
    padded = jnp.pad(field, ((1, 1), (0, 0), (0, 0)))

    def advance(totals, layer_index):
        colour, transmit = totals
        block = lax.dynamic_slice_in_dim(padded, layer_index, 3, 0)
        center = block[1]
        slope_depth = (block[2] - block[0]) * 0.5
        rows_pad = jnp.pad(center, ((1, 1), (0, 0)))
        slope_down = (rows_pad[2:] - rows_pad[:-2]) * 0.5
        cols_pad = jnp.pad(center, ((0, 0), (1, 1)))
        slope_across = (cols_pad[:, 2:] - cols_pad[:, :-2]) * 0.5
        layer_ids = lax.dynamic_index_in_dim(arc_ids, layer_index, 0, keepdims=False)
        looked = arc_params[:, layer_ids].astype(jnp.float32)
        passing, emitted = optics(center, slope_across, slope_down, slope_depth, looked, step_len)
        colour = colour + transmit[None] * emitted
        transmit = transmit * passing
        return ((colour, transmit), None)
    start_totals = (jnp.zeros((3, NY, NX), jnp.float32), jnp.ones((NY, NX), jnp.float32))
    final_totals, ignored = lax.scan(advance, start_totals, jnp.arange(NZ, dtype=jnp.int32))
    colour, transmit = final_totals
    return jnp.concatenate([colour, (1.0 - transmit)[None]], axis=0)
```

```python
import functools
import math

import jax
import jax.numpy as jnp
from jax import lax
from jax.experimental import pallas as pl
from jax.experimental.pallas import tpu as pltpu
from jax.sharding import PartitionSpec as P

LOG2E = math.log2(math.e)
SUB = 8
LANE = 128


def gathered(table, index):
    return jnp.take_along_axis(table, index, axis=1, mode="promise_in_bounds")


def fill_tables(arc_tf_ref, tf_ref, raw, arcs, tables, step_len):
    rows, tf_count = tf_ref.shape
    raw[...] = jnp.zeros_like(raw)
    raw[0:rows, 0:tf_count] = tf_ref[...].astype(jnp.float32)
    arcs[...] = jnp.zeros_like(arcs)
    arcs[0:1, 0 : arc_tf_ref.shape[1]] = arc_tf_ref[...]
    index = jnp.broadcast_to(arcs[0:1, :], (SUB, LANE))
    looked = [
        gathered(jnp.broadcast_to(raw[j : j + 1, :], (SUB, LANE)), index) for j in range(rows)
    ]
    for c in range(3):
        tables[c] = looked[c]
    tables[3] = looked[3] * (-step_len * LOG2E)
    tables[4] = looked[4]
    tables[5] = looked[5] * looked[5] * (-LOG2E)


def cast_kernel(
    step_len, field, ids, front, back, above, below, arc_tf, tf, part, vol, arc, raw, arcs, tables, sems
):
    depth, rows, columns = field.shape
    bands, strips = rows // SUB, columns // LANE

    def copies(band):
        span = pl.ds(band * SUB, SUB)
        return [
            pltpu.make_async_copy(
                field.at[:, span, :], vol.at[pl.ds(1, depth), span, :], sems.at[0, band]
            ),
            pltpu.make_async_copy(ids.at[:, span, :], arc.at[:, span, :], sems.at[1, band]),
        ]

    for band in range(bands):
        for copy in copies(band):
            copy.start()
    vol[0:1] = front[...]
    vol[depth + 1 : depth + 2] = back[...]
    fill_tables(arc_tf, tf, raw, arcs, tables, step_len)
    lane = lax.broadcasted_iota(jnp.int32, (SUB, LANE), 1)
    row = lax.broadcasted_iota(jnp.int32, (SUB, LANE), 0)
    first_lane, last_lane = lane == 0, lane == LANE - 1
    first_row, last_row = row == 0, row == SUB - 1
    zero = jnp.zeros((SUB, LANE), jnp.float32)

    for copy in copies(0):
        copy.wait()
    for band in range(bands):
        if band + 1 < bands:
            for copy in copies(band + 1):
                copy.wait()
        top = band * SUB

        def layer(z, totals, band=band, top=top):
            center = [vol[z + 1, top : top + SUB, s * LANE : (s + 1) * LANE] for s in range(strips)]
            to_right = [pltpu.roll(c, 1, 1) for c in center]
            to_left = [pltpu.roll(c, LANE - 1, 1) for c in center]
            out = []
            for s in range(strips):
                cols = slice(s * LANE, (s + 1) * LANE)
                c = center[s]
                left = jnp.where(first_lane, to_right[s - 1] if s else zero, to_right[s])
                right = jnp.where(last_lane, to_left[s + 1] if s + 1 < strips else zero, to_left[s])
                if band == 0:
                    over = above[z, 0:1, cols]
                else:
                    over = vol[z + 1, top - 1 : top, cols]
                if band == bands - 1:
                    under = below[z, 0:1, cols]
                else:
                    under = vol[z + 1, top + SUB : top + SUB + 1, cols]
                up = jnp.where(first_row, over, pltpu.roll(c, 1, 0))
                down = jnp.where(last_row, under, pltpu.roll(c, SUB - 1, 0))
                dx = right - left
                dy = down - up
                dz = vol[z + 2, top : top + SUB, cols] - vol[z, top : top + SUB, cols]
                slant = jnp.abs(0.312 * dx + 0.39 * dy + 0.416 * dz)
                shading = 0.35 + slant * lax.rsqrt(4.0 + dx * dx + dy * dy + dz * dz)
                index = arc[z, top : top + SUB, cols]
                looked = [gathered(tables[j], index) for j in range(6)]
                off = c - looked[4]
                passing = jnp.exp2(looked[3] * jnp.exp2(off * off * looked[5]))
                red, green, blue, transmit = totals[s]
                after = transmit * passing
                weight = (transmit - after) * shading
                out.append(
                    (
                        red + weight * looked[0],
                        green + weight * looked[1],
                        blue + weight * looked[2],
                        after,
                    )
                )
            return tuple(out)

        start = tuple((zero, zero, zero, zero + 1.0) for _ in range(strips))
        totals = lax.fori_loop(0, depth, layer, start, unroll=2)
        for s in range(strips):
            for j in range(4):
                part[band * strips + s, j] = totals[s][j]


def merge_kernel(parts, out):
    count = parts.shape[0]
    red, green, blue, transmit = (parts[0, j] for j in range(4))
    for s in range(1, count):
        red = red + transmit * parts[s, 0]
        green = green + transmit * parts[s, 1]
        blue = blue + transmit * parts[s, 2]
        transmit = transmit * parts[s, 3]
    for s in range(count):
        for j, value in enumerate((red, green, blue, 1.0 - transmit)):
            out[s, j] = value


def shifted(value, axis, step):
    count = lax.axis_size(axis)
    return lax.ppermute(
        value, axis, [(i, i + step) for i in range(count) if 0 <= i + step < count]
    )


def local(field, arc_ids, arc_tf, tf_table):
    depth, rows, columns = field.shape
    slabs = lax.axis_size("slab")
    bands, strips = rows // SUB, columns // LANE
    above = shifted(field[:, rows - 1 :, :], "tile", 1)
    below = shifted(field[:, :1, :], "tile", -1)
    front = shifted(field[depth - 1 :], "slab", 1)
    back = shifted(field[:1], "slab", -1)
    vmem = pl.BlockSpec(memory_space=pltpu.VMEM)
    hbm = pl.BlockSpec(memory_space=pl.ANY)
    parts = pl.pallas_call(
        functools.partial(cast_kernel, 2.0 / (depth * slabs)),
        out_shape=jax.ShapeDtypeStruct((bands * strips, 4, SUB, LANE), jnp.float32),
        in_specs=[hbm, hbm] + [vmem] * 6,
        out_specs=vmem,
        scratch_shapes=[
            pltpu.VMEM((depth + 2, rows, columns), jnp.float32),
            pltpu.VMEM((depth, rows, columns), jnp.int32),
            pltpu.VMEM((SUB, LANE), jnp.float32),
            pltpu.VMEM((SUB, LANE), jnp.int32),
            pltpu.VMEM((6, SUB, LANE), jnp.float32),
            pltpu.SemaphoreType.DMA((2, bands)),
        ],
        compiler_params=pltpu.CompilerParams(vmem_limit_bytes=16 * 2**20),
        name="cast",
    )(field, arc_ids, front, back, above, below, arc_tf[None, :], tf_table)
    received = lax.all_to_all(parts, "slab", 0, 0, tiled=True)
    merged = pl.pallas_call(
        merge_kernel,
        out_shape=jax.ShapeDtypeStruct((slabs, 4, SUB, LANE), jnp.float32),
        in_specs=[vmem],
        out_specs=vmem,
        name="merge",
    )(received)
    pixels = lax.all_to_all(merged, "slab", 0, 0, tiled=True)
    pixels = pixels.reshape(bands, strips, 4, SUB, LANE).transpose(2, 0, 3, 1, 4)
    return pixels.reshape(4, rows, columns)


def solution(mesh):
    in_specs = (P("slab", "tile", None), P("slab", "tile", None), P(), P())
    out_specs = P(None, "tile", None)
    return jax.shard_map(local, mesh=mesh, in_specs=in_specs, out_specs=out_specs, check_vma=False)
```

```python
import functools
import math

import jax
import jax.numpy as jnp
from jax import lax
from jax.experimental import pallas as pl
from jax.experimental.pallas import tpu as pltpu
from jax.sharding import PartitionSpec as P

LOG2E = math.log2(math.e)
SUB = 8
LANE = 128
ALONG_LANES = lax.GatherDimensionNumbers(
    offset_dims=(),
    collapsed_slice_dims=(1,),
    start_index_map=(1,),
    operand_batching_dims=(0,),
    start_indices_batching_dims=(0,),
)
FRACTION = 2.0**30
GREEN_TOP = 2**16 - 1
WIDTH_TOP = 2**10 - 1
FINE = 512.0
CENTRE_UNIT = 2.0**-29
EXTINCTION_SPAN = 2**13


def gathered(table, index):
    return lax.gather(
        table, index[:, :, None], ALONG_LANES, (1, 1), mode=lax.GatherScatterMode.PROMISE_IN_BOUNDS
    )


def whole(value):
    return jnp.floor(value + 0.5).astype(jnp.int32)


def word(high, low, low_span):
    return whole((high - low.astype(jnp.float32)) / low_span) * low_span + low


def fill_tables(arc_tf, tf, raw, arcs, words):
    rows, tf_count = tf.shape
    raw[...] = jnp.zeros_like(raw)
    raw[0:rows, 0:tf_count] = tf[...].astype(jnp.float32)
    arcs[...] = jnp.zeros_like(arcs)
    arcs[0:1, 0 : arc_tf.shape[1]] = arc_tf[...]
    index = jnp.broadcast_to(arcs[0:1, :], (SUB, LANE))
    red, green, blue, extinction, centre, width = [
        gathered(jnp.broadcast_to(raw[j : j + 1, :], (SUB, LANE)), index) for j in range(rows)
    ]
    words[0] = word(red * FRACTION, whole(green * GREEN_TOP), GREEN_TOP + 1)
    words[1] = word(blue * FRACTION, whole(width * FINE), WIDTH_TOP + 1)
    words[2] = word(
        centre / CENTRE_UNIT, EXTINCTION_SPAN - whole(extinction * FINE), EXTINCTION_SPAN
    )


def compose(step_len, vol, arc, words, top, layers, front, back, above, below, totals):
    depth, rows, columns = vol.shape
    strips = columns // LANE
    band = pl.ds(top, SUB)
    lane = lax.broadcasted_iota(jnp.int32, (SUB, LANE), 1)
    row = lax.broadcasted_iota(jnp.int32, (SUB, LANE), 0)
    first_lane, last_lane = lane == 0, lane == LANE - 1
    first_row, last_row = row == 0, row == SUB - 1
    zero = jnp.zeros((SUB, LANE), jnp.float32)
    log_step = math.log2(step_len * LOG2E / FINE)
    totals = list(totals)
    for z in layers:
        center = [vol[z, band, s * LANE : (s + 1) * LANE] for s in range(strips)]
        to_right = [pltpu.roll(c, 1, 1) for c in center]
        to_left = [pltpu.roll(c, LANE - 1, 1) for c in center]
        for s in range(strips):
            cols = slice(s * LANE, (s + 1) * LANE)
            c = center[s]
            index = arc[z, band, cols]
            red_green, blue_width, centre_ext = [gathered(words[j], index) for j in range(3)]
            off = c - centre_ext.astype(jnp.float32) * CENTRE_UNIT
            reach = off * (blue_width & WIDTH_TOP).astype(jnp.float32)
            bell = jnp.exp2(reach * reach * (-LOG2E / FINE**2) + log_step)
            passing = jnp.exp2((centre_ext | -EXTINCTION_SPAN).astype(jnp.float32) * bell)

            left = jnp.where(first_lane, to_right[s - 1] if s else zero, to_right[s])
            right = jnp.where(last_lane, to_left[s + 1] if s + 1 < strips else zero, to_left[s])
            over = above[z, 0:1, cols] if above is not None else vol[z, pl.ds(top - SUB, SUB), cols]
            under = below[z, 0:1, cols] if below is not None else vol[z, pl.ds(top + SUB, SUB), cols]
            up = pltpu.roll(jnp.where(last_row, over, c), 1, 0)
            down = pltpu.roll(jnp.where(first_row, under, c), SUB - 1, 0)
            nearer = vol[z - 1, band, cols] if z else front[0, band, cols]
            farther = vol[z + 1, band, cols] if z + 1 < depth else back[0, band, cols]
            dx = right - left
            dy = down - up
            dz = farther - nearer
            slant = jnp.abs(0.312 * dx + 0.39 * dy + 0.416 * dz)
            shading = 0.35 + slant * lax.rsqrt(4.0 + dx * dx + dy * dy + dz * dz)

            red, green, blue, transmit = totals[s]
            after = transmit * passing
            weight = (transmit - after) * shading
            totals[s] = (
                red + weight * red_green.astype(jnp.float32),
                green + weight * (red_green & GREEN_TOP).astype(jnp.float32),
                blue + weight * blue_width.astype(jnp.float32),
                after,
            )
    return totals


def clear(strips):
    zero = jnp.zeros((SUB, LANE), jnp.float32)
    return [(zero, zero, zero, zero + 1.0)] * strips


def faces_kernel(field, first, last, top, bottom, top_band, bottom_band, sems):
    depth, rows, columns = field.shape
    copies = [
        pltpu.make_async_copy(field.at[depth - 1 :], last, sems.at[0]),
        pltpu.make_async_copy(field.at[:1], first, sems.at[1]),
        pltpu.make_async_copy(field.at[:, rows - SUB :, :], bottom_band, sems.at[2]),
        pltpu.make_async_copy(field.at[:, :SUB, :], top_band, sems.at[3]),
    ]
    for copy in copies:
        copy.start()
    for copy in copies:
        copy.wait()
    top[...] = top_band[:, 0:1, :]
    bottom[...] = bottom_band[:, SUB - 1 :, :]


def cast_kernel(
    step_len,
    field,
    ids,
    arc_tf,
    tf,
    front,
    back,
    above,
    below,
    parts,
    vol,
    arc,
    arc_tf_here,
    tf_here,
    raw,
    arcs,
    words,
    sems,
):
    depth, rows, columns = field.shape
    bands, strips = rows // SUB, columns // LANE

    def copies(band):
        span = pl.ds(pl.multiple_of(band * SUB, SUB), SUB)
        return [
            pltpu.make_async_copy(field.at[:, span, :], vol.at[:, span, :], sems.at[0, band]),
            pltpu.make_async_copy(ids.at[:, span, :], arc.at[:, span, :], sems.at[1, band]),
        ]

    small = [
        pltpu.make_async_copy(arc_tf, arc_tf_here, sems.at[2, 0]),
        pltpu.make_async_copy(tf, tf_here, sems.at[2, 1]),
    ]
    for copy in small:
        copy.start()
    for band in range(bands):
        for copy in copies(band):
            copy.start()
    for copy in small:
        copy.wait()
    fill_tables(arc_tf_here, tf_here, raw, arcs, words)
    slab, tile = lax.axis_index("slab"), lax.axis_index("tile")
    front[...] = front[...] * (slab > 0).astype(jnp.float32)
    back[...] = back[...] * (slab < lax.axis_size("slab") - 1).astype(jnp.float32)
    above[...] = above[...] * (tile > 0).astype(jnp.float32)
    below[...] = below[...] * (tile < lax.axis_size("tile") - 1).astype(jnp.float32)
    scale = (1.0 / FRACTION, 1.0 / GREEN_TOP, 1.0 / FRACTION, 1.0)

    def work(band, over, under):
        top = pl.multiple_of(band * SUB, SUB)
        totals = compose(
            step_len, vol, arc, words, top, range(depth), front, back, over, under, clear(strips)
        )
        for s in range(strips):
            for j in range(4):
                parts[band * strips + s, j] = totals[s][j] * scale[j]

    for copy in copies(0) + copies(1):
        copy.wait()
    work(0, above, None)

    def step(band, carry):
        for copy in copies(band + 1):
            copy.wait()
        work(band, None, None)
        return carry

    lax.fori_loop(1, bands - 1, step, 0)
    work(bands - 1, None, below)


def merge_kernel(parts, out):
    count = parts.shape[0]
    red, green, blue, transmit = (parts[0, j] for j in range(4))
    for s in range(1, count):
        red = red + transmit * parts[s, 0]
        green = green + transmit * parts[s, 1]
        blue = blue + transmit * parts[s, 2]
        transmit = transmit * parts[s, 3]
    for s in range(count):
        for j, value in enumerate((red, green, blue, 1.0 - transmit)):
            out[s, j] = value


def shifted(value, axis, step):
    count = lax.axis_size(axis)
    if axis == "tile":
        return lax.ppermute(value, axis, [(i, (i + step) % count) for i in range(count)])
    return lax.ppermute(
        value, axis, [(i, i + step) for i in range(count) if 0 <= i + step < count]
    )


def local(field, arc_ids, arc_tf, tf_table):
    depth, rows, columns = field.shape
    slabs = lax.axis_size("slab")
    step_len = 2.0 / (depth * slabs)
    bands, strips = rows // SUB, columns // LANE
    f32 = jnp.float32
    vmem = pl.BlockSpec(memory_space=pltpu.VMEM)
    hbm = pl.BlockSpec(memory_space=pltpu.HBM)
    shape = jax.ShapeDtypeStruct
    band_shape = (depth, SUB, columns)
    first, last, top, bottom = pl.pallas_call(
        faces_kernel,
        out_shape=[shape((1, rows, columns), f32)] * 2 + [shape((depth, 1, columns), f32)] * 2,
        in_specs=[hbm],
        out_specs=[vmem] * 4,
        scratch_shapes=[pltpu.VMEM(band_shape, f32)] * 2 + [pltpu.SemaphoreType.DMA((4,))],
        compiler_params=pltpu.CompilerParams(vmem_limit_bytes=52 * 2**20),
        name="faces",
    )(field)
    front = shifted(last, "slab", 1)
    back = shifted(first, "slab", -1)
    above = shifted(bottom, "tile", 1)
    below = shifted(top, "tile", -1)
    parts = pl.pallas_call(
        functools.partial(cast_kernel, step_len),
        out_shape=shape((bands * strips, 4, SUB, LANE), f32),
        in_specs=[hbm] * 4 + [vmem] * 4,
        out_specs=vmem,
        scratch_shapes=[
            pltpu.VMEM(field.shape, f32),
            pltpu.VMEM(field.shape, jnp.int32),
            pltpu.VMEM((1, arc_tf.shape[0]), jnp.int32),
            pltpu.VMEM(tf_table.shape, tf_table.dtype),
            pltpu.VMEM((SUB, LANE), f32),
            pltpu.VMEM((SUB, LANE), jnp.int32),
            pltpu.VMEM((3, SUB, LANE), jnp.int32),
            pltpu.SemaphoreType.DMA((3, max(bands, 2))),
        ],
        compiler_params=pltpu.CompilerParams(vmem_limit_bytes=52 * 2**20),
        name="cast",
    )(field, arc_ids, arc_tf[None, :], tf_table, front, back, above, below)
    received = lax.all_to_all(parts, "slab", 0, 0, tiled=True)
    merged = pl.pallas_call(
        merge_kernel,
        out_shape=shape((slabs, 4, SUB, LANE), f32),
        in_specs=[vmem],
        out_specs=vmem,
        compiler_params=pltpu.CompilerParams(vmem_limit_bytes=4 * 2**20),
        name="merge",
    )(received)
    pixels = lax.all_to_all(merged, "slab", 0, 0, tiled=True)
    pixels = pixels.reshape(bands, strips, 4, SUB, LANE).transpose(2, 0, 3, 1, 4)
    return pixels.reshape(4, rows, columns)


def solution(mesh):
    in_specs = (P("slab", "tile", None), P("slab", "tile", None), P(), P())
    out_specs = P(None, "tile", None)
    return jax.shard_map(local, mesh=mesh, in_specs=in_specs, out_specs=out_specs, check_vma=False)
```

```python
import functools
import math

import jax
import jax.numpy as jnp
from jax import lax
from jax.experimental import pallas as pl
from jax.experimental.pallas import tpu as pltpu
from jax.sharding import PartitionSpec as P

LOG2E = math.log2(math.e)
SUB = 8
LANE = 128
ALONG_LANES = lax.GatherDimensionNumbers(
    offset_dims=(),
    collapsed_slice_dims=(1,),
    start_index_map=(1,),
    operand_batching_dims=(0,),
    start_indices_batching_dims=(0,),
)
FRACTION = 2.0**30
GREEN_TOP = 2**16 - 1
WIDTH_TOP = 2**10 - 1
FINE = 512.0
CENTRE_UNIT = 2.0**-29
EXTINCTION_SPAN = 2**13


def gathered(table, index):
    return lax.gather(
        table, index[:, :, None], ALONG_LANES, (1, 1), mode=lax.GatherScatterMode.PROMISE_IN_BOUNDS
    )


def whole(value):
    return jnp.floor(value + 0.5).astype(jnp.int32)


def word(high, low, low_span):
    return whole((high - low.astype(jnp.float32)) / low_span) * low_span + low


def fill_tables(arc_tf, tf, raw, arcs, words):
    rows, tf_count = tf.shape
    raw[...] = jnp.zeros_like(raw)
    raw[0:rows, 0:tf_count] = tf[...].astype(jnp.float32)
    arcs[...] = jnp.zeros_like(arcs)
    arcs[0:1, 0 : arc_tf.shape[1]] = arc_tf[...]
    index = jnp.broadcast_to(arcs[0:1, :], (SUB, LANE))
    red, green, blue, extinction, centre, width = [
        gathered(jnp.broadcast_to(raw[j : j + 1, :], (SUB, LANE)), index) for j in range(rows)
    ]
    words[0] = word(red * FRACTION, whole(green * GREEN_TOP), GREEN_TOP + 1)
    words[1] = word(blue * FRACTION, whole(width * FINE), WIDTH_TOP + 1)
    words[2] = word(
        centre / CENTRE_UNIT, EXTINCTION_SPAN - whole(extinction * FINE), EXTINCTION_SPAN
    )


def compose(step_len, vol, arc, words, top, layers, front, back, above, below, totals):
    depth, rows, columns = vol.shape
    strips = columns // LANE
    band = pl.ds(top, SUB)
    lane = lax.broadcasted_iota(jnp.int32, (SUB, LANE), 1)
    row = lax.broadcasted_iota(jnp.int32, (SUB, LANE), 0)
    first_lane, last_lane = lane == 0, lane == LANE - 1
    first_row, last_row = row == 0, row == SUB - 1
    zero = jnp.zeros((SUB, LANE), jnp.float32)
    log_step = math.log2(step_len * LOG2E / FINE)
    totals = list(totals)
    for z in layers:
        center = [vol[z, band, s * LANE : (s + 1) * LANE] for s in range(strips)]
        to_right = [pltpu.roll(c, 1, 1) for c in center]
        to_left = [pltpu.roll(c, LANE - 1, 1) for c in center]
        for s in range(strips):
            cols = slice(s * LANE, (s + 1) * LANE)
            c = center[s]
            index = arc[z, band, cols]
            red_green, blue_width, centre_ext = [gathered(words[j], index) for j in range(3)]
            off = c - centre_ext.astype(jnp.float32) * CENTRE_UNIT
            reach = off * (blue_width & WIDTH_TOP).astype(jnp.float32)
            bell = jnp.exp2(reach * reach * (-LOG2E / FINE**2) + log_step)
            passing = jnp.exp2((centre_ext | -EXTINCTION_SPAN).astype(jnp.float32) * bell)

            left = jnp.where(first_lane, to_right[s - 1] if s else zero, to_right[s])
            right = jnp.where(last_lane, to_left[s + 1] if s + 1 < strips else zero, to_left[s])
            over = above[z, 0:1, cols] if above is not None else vol[z, pl.ds(top - SUB, SUB), cols]
            under = below[z, 0:1, cols] if below is not None else vol[z, pl.ds(top + SUB, SUB), cols]
            up = pltpu.roll(jnp.where(last_row, over, c), 1, 0)
            down = pltpu.roll(jnp.where(first_row, under, c), SUB - 1, 0)
            nearer = vol[z - 1, band, cols] if z else front[0, band, cols]
            farther = vol[z + 1, band, cols] if z + 1 < depth else back[0, band, cols]
            dx = right - left
            dy = down - up
            dz = farther - nearer
            slant = jnp.abs(0.312 * dx + 0.39 * dy + 0.416 * dz)
            shading = 0.35 + slant * lax.rsqrt(4.0 + dx * dx + dy * dy + dz * dz)

            red, green, blue, transmit = totals[s]
            after = transmit * passing
            weight = (transmit - after) * shading
            totals[s] = (
                red + weight * red_green.astype(jnp.float32),
                green + weight * (red_green & GREEN_TOP).astype(jnp.float32),
                blue + weight * blue_width.astype(jnp.float32),
                after,
            )
    return totals


def clear(strips):
    zero = jnp.zeros((SUB, LANE), jnp.float32)
    return [(zero, zero, zero, zero + 1.0)] * strips


def faces_kernel(field, first, last, top, bottom):
    depth, rows, columns = field.shape
    last[...] = field[depth - 1 :]
    first[...] = field[:1]
    top[...] = field[:, 0:1, :]
    bottom[...] = field[:, rows - 1 :, :]


def inner_kernel(step_len, vol, arc, arc_tf, tf, words, inner, raw, arcs):
    depth, rows, columns = vol.shape
    bands, strips = rows // SUB, columns // LANE
    fill_tables(arc_tf, tf, raw, arcs, words)

    def step(band, carry):
        top = pl.multiple_of(band * SUB, SUB)
        totals = compose(
            step_len, vol, arc, words, top, range(1, depth - 1), None, None, None, None, clear(strips)
        )
        for s in range(strips):
            for j in range(4):
                inner[(band - 1) * strips + s, j] = totals[s][j]
        return carry

    lax.fori_loop(1, bands - 1, step, 0, unroll=3 if (bands - 2) % 3 == 0 else 1)


def outer_kernel(step_len, vol, arc, words, inner, front, back, above, below, parts):
    depth, rows, columns = vol.shape
    bands, strips = rows // SUB, columns // LANE
    slab, tile = lax.axis_index("slab"), lax.axis_index("tile")
    front[...] = front[...] * (slab > 0).astype(jnp.float32)
    back[...] = back[...] * (slab < lax.axis_size("slab") - 1).astype(jnp.float32)
    above[...] = above[...] * (tile > 0).astype(jnp.float32)
    below[...] = below[...] * (tile < lax.axis_size("tile") - 1).astype(jnp.float32)
    scale = (1.0 / FRACTION, 1.0 / GREEN_TOP, 1.0 / FRACTION, 1.0)

    def put(band, totals):
        for s in range(strips):
            for j in range(4):
                parts[band * strips + s, j] = totals[s][j] * scale[j]

    def whole_band(band, over, under):
        top = band * SUB
        put(
            band,
            compose(
                step_len, vol, arc, words, top, range(depth), front, back, over, under, clear(strips)
            ),
        )

    def step(band, carry):
        top = pl.multiple_of(band * SUB, SUB)
        at = (step_len, vol, arc, words, top)
        totals = compose(*at, [0], front, back, None, None, clear(strips))
        for s in range(strips):
            red, green, blue, transmit = totals[s]
            behind = [inner[(band - 1) * strips + s, j] for j in range(4)]
            totals[s] = (
                red + transmit * behind[0],
                green + transmit * behind[1],
                blue + transmit * behind[2],
                transmit * behind[3],
            )
        put(band, compose(*at, [depth - 1], front, back, None, None, totals))
        return carry

    lax.fori_loop(1, bands - 1, step, 0, unroll=3 if (bands - 2) % 3 == 0 else 1)
    whole_band(0, above, None)
    whole_band(bands - 1, None, below)


def merge_kernel(parts, out):
    count = parts.shape[0]
    red, green, blue, transmit = (parts[0, j] for j in range(4))
    for s in range(1, count):
        red = red + transmit * parts[s, 0]
        green = green + transmit * parts[s, 1]
        blue = blue + transmit * parts[s, 2]
        transmit = transmit * parts[s, 3]
    for s in range(count):
        for j, value in enumerate((red, green, blue, 1.0 - transmit)):
            out[s, j] = value


def shifted(value, axis, step):
    count = lax.axis_size(axis)
    if axis == "tile":
        return lax.ppermute(value, axis, [(i, (i + step) % count) for i in range(count)])
    return lax.ppermute(
        value, axis, [(i, i + step) for i in range(count) if 0 <= i + step < count]
    )


def local(field, arc_ids, arc_tf, tf_table):
    depth, rows, columns = field.shape
    slabs = lax.axis_size("slab")
    step_len = 2.0 / (depth * slabs)
    bands, strips = rows // SUB, columns // LANE
    f32 = jnp.float32
    vmem = pl.BlockSpec(memory_space=pltpu.VMEM)
    hbm = pl.BlockSpec(memory_space=pltpu.HBM)
    shape = jax.ShapeDtypeStruct
    first, last, top, bottom = pl.pallas_call(
        faces_kernel,
        out_shape=[shape((1, rows, columns), f32)] * 2 + [shape((depth, 1, columns), f32)] * 2,
        in_specs=[vmem],
        out_specs=[vmem] * 4,
        compiler_params=pltpu.CompilerParams(vmem_limit_bytes=40 * 2**20),
        name="faces",
    )(field)
    front = shifted(last, "slab", 1)
    back = shifted(first, "slab", -1)
    above = shifted(bottom, "tile", 1)
    below = shifted(top, "tile", -1)
    words, inner = pl.pallas_call(
        functools.partial(inner_kernel, step_len),
        out_shape=[
            shape((3, SUB, LANE), jnp.int32),
            shape(((bands - 2) * strips, 4, SUB, LANE), f32),
        ],
        in_specs=[vmem] * 4,
        out_specs=[vmem] * 2,
        scratch_shapes=[pltpu.VMEM((SUB, LANE), f32), pltpu.VMEM((SUB, LANE), jnp.int32)],
        compiler_params=pltpu.CompilerParams(vmem_limit_bytes=12 * 2**20),
        cost_estimate=pl.CostEstimate(
            flops=60 * field.size, bytes_accessed=8 * field.size, transcendentals=3 * field.size
        ),
        name="inner",
    )(field, arc_ids, arc_tf[None, :], tf_table)
    parts = pl.pallas_call(
        functools.partial(outer_kernel, step_len),
        out_shape=shape((bands * strips, 4, SUB, LANE), f32),
        in_specs=[vmem] * 8,
        out_specs=vmem,
        compiler_params=pltpu.CompilerParams(vmem_limit_bytes=12 * 2**20),
        name="outer",
    )(field, arc_ids, words, inner, front, back, above, below)
    received = lax.all_to_all(parts, "slab", 0, 0, tiled=True)
    merged = pl.pallas_call(
        merge_kernel,
        out_shape=shape((slabs, 4, SUB, LANE), f32),
        in_specs=[vmem],
        out_specs=vmem,
        compiler_params=pltpu.CompilerParams(vmem_limit_bytes=4 * 2**20),
        name="merge",
    )(received)
    pixels = lax.all_to_all(merged, "slab", 0, 0, tiled=True)
    pixels = pixels.reshape(bands, strips, 4, SUB, LANE).transpose(2, 0, 3, 1, 4)
    return pixels.reshape(4, rows, columns)


def solution(mesh):
    in_specs = (P("slab", "tile", None), P("slab", "tile", None), P(), P())
    out_specs = P(None, "tile", None)
    return jax.shard_map(local, mesh=mesh, in_specs=in_specs, out_specs=out_specs, check_vma=False)
```

```python
import functools
import math

import jax
import jax.numpy as jnp
from jax import lax
from jax.experimental import pallas as pl
from jax.experimental.pallas import tpu as pltpu
from jax.sharding import PartitionSpec as P

LOG2E = math.log2(math.e)
SUB = 8
LANE = 128
ALONG_LANES = lax.GatherDimensionNumbers(
    offset_dims=(),
    collapsed_slice_dims=(1,),
    start_index_map=(1,),
    operand_batching_dims=(0,),
    start_indices_batching_dims=(0,),
)
FRACTION = 2.0**30
GREEN_TOP = 2**16 - 1
WIDTH_TOP = 2**10 - 1
FINE = 512.0
CENTRE_UNIT = 2.0**-29
EXTINCTION_SPAN = 2**13


def gathered(table, index):
    return lax.gather(
        table, index[:, :, None], ALONG_LANES, (1, 1), mode=lax.GatherScatterMode.PROMISE_IN_BOUNDS
    )


def whole(value):
    return jnp.floor(value + 0.5).astype(jnp.int32)


def word(high, low, low_span):
    return whole((high - low.astype(jnp.float32)) / low_span) * low_span + low


def fill_tables(arc_tf, tf, raw, arcs, words):
    rows, tf_count = tf.shape
    raw[...] = jnp.zeros_like(raw)
    raw[0:rows, 0:tf_count] = tf[...].astype(jnp.float32)
    arcs[...] = jnp.zeros_like(arcs)
    arcs[0:1, 0 : arc_tf.shape[1]] = arc_tf[...]
    index = jnp.broadcast_to(arcs[0:1, :], (SUB, LANE))
    red, green, blue, extinction, centre, width = [
        gathered(jnp.broadcast_to(raw[j : j + 1, :], (SUB, LANE)), index) for j in range(rows)
    ]
    words[0] = word(red * FRACTION, whole(green * GREEN_TOP), GREEN_TOP + 1)
    words[1] = word(blue * FRACTION, whole(width * FINE), WIDTH_TOP + 1)
    words[2] = word(
        centre / CENTRE_UNIT, EXTINCTION_SPAN - whole(extinction * FINE), EXTINCTION_SPAN
    )


def compose(step_len, vol, arc, words, top, layers, front, back, above, below, totals):
    depth, rows, columns = vol.shape
    strips = columns // LANE
    band = pl.ds(top, SUB)
    lane = lax.broadcasted_iota(jnp.int32, (SUB, LANE), 1)
    row = lax.broadcasted_iota(jnp.int32, (SUB, LANE), 0)
    first_lane, last_lane = lane == 0, lane == LANE - 1
    first_row, last_row = row == 0, row == SUB - 1
    zero = jnp.zeros((SUB, LANE), jnp.float32)
    log_step = math.log2(step_len * LOG2E / FINE)
    totals = list(totals)
    for z in layers:
        center = [vol[z, band, s * LANE : (s + 1) * LANE] for s in range(strips)]
        to_right = [pltpu.roll(c, 1, 1) for c in center]
        to_left = [pltpu.roll(c, LANE - 1, 1) for c in center]
        for s in range(strips):
            cols = slice(s * LANE, (s + 1) * LANE)
            c = center[s]
            index = arc[z, band, cols]
            red_green, blue_width, centre_ext = [gathered(words[j], index) for j in range(3)]
            off = c - centre_ext.astype(jnp.float32) * CENTRE_UNIT
            reach = off * (blue_width & WIDTH_TOP).astype(jnp.float32)
            bell = jnp.exp2(reach * reach * (-LOG2E / FINE**2) + log_step)
            passing = jnp.exp2((centre_ext | -EXTINCTION_SPAN).astype(jnp.float32) * bell)

            left = jnp.where(first_lane, to_right[s - 1] if s else zero, to_right[s])
            right = jnp.where(last_lane, to_left[s + 1] if s + 1 < strips else zero, to_left[s])
            over = above[z, 0:1, cols] if above is not None else vol[z, pl.ds(top - SUB, SUB), cols]
            under = below[z, 0:1, cols] if below is not None else vol[z, pl.ds(top + SUB, SUB), cols]
            up = pltpu.roll(jnp.where(last_row, over, c), 1, 0)
            down = pltpu.roll(jnp.where(first_row, under, c), SUB - 1, 0)
            nearer = vol[z - 1, band, cols] if z else front[0, band, cols]
            farther = vol[z + 1, band, cols] if z + 1 < depth else back[0, band, cols]
            dx = right - left
            dy = down - up
            dz = farther - nearer
            slant = jnp.abs(0.312 * dx + 0.39 * dy + 0.416 * dz)
            shading = 0.35 + slant * lax.rsqrt(4.0 + dx * dx + dy * dy + dz * dz)

            red, green, blue, transmit = totals[s]
            after = transmit * passing
            weight = (transmit - after) * shading
            totals[s] = (
                red + weight * red_green.astype(jnp.float32),
                green + weight * (red_green & GREEN_TOP).astype(jnp.float32),
                blue + weight * blue_width.astype(jnp.float32),
                after,
            )
    return totals


def clear(strips):
    zero = jnp.zeros((SUB, LANE), jnp.float32)
    return [(zero, zero, zero, zero + 1.0)] * strips


def faces_kernel(field, layer_1, layer_2, top, bottom):
    depth, rows, columns = field.shape
    slab_odd = lax.axis_index("slab") % 2
    layer_1[...] = field[pl.ds((1 - slab_odd) * (depth - 1), 1)]
    layer_2[...] = field[pl.ds(slab_odd * (depth - 1), 1)]
    top[...] = field[:, 0:1, :]
    bottom[...] = field[:, rows - 1 :, :]


def inner_kernel(step_len, vol, arc, arc_tf, tf, words, inner, raw, arcs):
    depth, rows, columns = vol.shape
    bands, strips = rows // SUB, columns // LANE
    fill_tables(arc_tf, tf, raw, arcs, words)

    def step(band, carry):
        top = pl.multiple_of(band * SUB, SUB)
        totals = compose(
            step_len, vol, arc, words, top, range(1, depth - 1), None, None, None, None, clear(strips)
        )
        for s in range(strips):
            for j in range(4):
                inner[(band - 1) * strips + s, j] = totals[s][j]
        return carry

    lax.fori_loop(1, bands - 1, step, 0, unroll=3 if (bands - 2) % 3 == 0 else 1)


def outer_kernel(step_len, vol, arc, words, inner, layer_1, layer_2, above, below, parts, halo):
    depth, rows, columns = vol.shape
    bands, strips = rows // SUB, columns // LANE
    slab, tile = lax.axis_index("slab"), lax.axis_index("tile")
    slab_odd = slab % 2
    slab_inner = (slab > 0) & (slab < lax.axis_size("slab") - 1)
    halo[pl.ds(1 - slab_odd, 1)] = layer_1[...]
    halo[pl.ds(slab_odd, 1)] = layer_2[...] * slab_inner.astype(jnp.float32)
    front, back = halo.at[0:1], halo.at[1:2]
    above[...] = above[...] * (tile > 0).astype(jnp.float32)
    below[...] = below[...] * (tile < lax.axis_size("tile") - 1).astype(jnp.float32)
    scale = (1.0 / FRACTION, 1.0 / GREEN_TOP, 1.0 / FRACTION, 1.0)

    def put(band, totals):
        for s in range(strips):
            for j in range(4):
                parts[band * strips + s, j] = totals[s][j] * scale[j]

    def whole_band(band, over, under):
        top = band * SUB
        put(
            band,
            compose(
                step_len, vol, arc, words, top, range(depth), front, back, over, under, clear(strips)
            ),
        )

    def step(band, carry):
        top = pl.multiple_of(band * SUB, SUB)
        at = (step_len, vol, arc, words, top)
        totals = compose(*at, [0], front, back, None, None, clear(strips))
        for s in range(strips):
            red, green, blue, transmit = totals[s]
            behind = [inner[(band - 1) * strips + s, j] for j in range(4)]
            totals[s] = (
                red + transmit * behind[0],
                green + transmit * behind[1],
                blue + transmit * behind[2],
                transmit * behind[3],
            )
        put(band, compose(*at, [depth - 1], front, back, None, None, totals))
        return carry

    lax.fori_loop(1, bands - 1, step, 0, unroll=3 if (bands - 2) % 3 == 0 else 1)
    whole_band(0, above, None)
    whole_band(bands - 1, None, below)


def merge_kernel(parts, out):
    count = parts.shape[0]
    red, green, blue, transmit = (parts[0, j] for j in range(4))
    for s in range(1, count):
        red = red + transmit * parts[s, 0]
        green = green + transmit * parts[s, 1]
        blue = blue + transmit * parts[s, 2]
        transmit = transmit * parts[s, 3]
    for s in range(count):
        for j, value in enumerate((red, green, blue, 1.0 - transmit)):
            out[s, j] = value


def shifted(value, axis, step):
    count = lax.axis_size(axis)
    if axis == "tile":
        return lax.ppermute(value, axis, [(i, (i + step) % count) for i in range(count)])
    return lax.ppermute(
        value, axis, [(i, i + step) for i in range(count) if 0 <= i + step < count]
    )


def swapped(value, axis, first):
    count = lax.axis_size(axis)
    partner = {i: i for i in range(count)}
    for i in range(first, count - 1, 2):
        partner[i], partner[i + 1] = i + 1, i
    return lax.ppermute(value, axis, list(partner.items()))


def local(field, arc_ids, arc_tf, tf_table):
    depth, rows, columns = field.shape
    slabs = lax.axis_size("slab")
    step_len = 2.0 / (depth * slabs)
    bands, strips = rows // SUB, columns // LANE
    f32 = jnp.float32
    vmem = pl.BlockSpec(memory_space=pltpu.VMEM)
    hbm = pl.BlockSpec(memory_space=pltpu.HBM)
    shape = jax.ShapeDtypeStruct
    layer_1, layer_2, top, bottom = pl.pallas_call(
        faces_kernel,
        out_shape=[shape((1, rows, columns), f32)] * 2 + [shape((depth, 1, columns), f32)] * 2,
        in_specs=[vmem],
        out_specs=[vmem] * 4,
        compiler_params=pltpu.CompilerParams(vmem_limit_bytes=40 * 2**20),
        name="faces",
    )(field)
    layer_2 = swapped(layer_2, "slab", 1)
    layer_1 = swapped(layer_1, "slab", 0)
    above = shifted(bottom, "tile", 1)
    below = shifted(top, "tile", -1)
    words, inner = pl.pallas_call(
        functools.partial(inner_kernel, step_len),
        out_shape=[
            shape((3, SUB, LANE), jnp.int32),
            shape(((bands - 2) * strips, 4, SUB, LANE), f32),
        ],
        in_specs=[vmem] * 4,
        out_specs=[vmem] * 2,
        scratch_shapes=[pltpu.VMEM((SUB, LANE), f32), pltpu.VMEM((SUB, LANE), jnp.int32)],
        compiler_params=pltpu.CompilerParams(vmem_limit_bytes=12 * 2**20),
        cost_estimate=pl.CostEstimate(
            flops=60 * field.size, bytes_accessed=8 * field.size, transcendentals=3 * field.size
        ),
        name="inner",
    )(field, arc_ids, arc_tf[None, :], tf_table)
    parts = pl.pallas_call(
        functools.partial(outer_kernel, step_len),
        out_shape=shape((bands * strips, 4, SUB, LANE), f32),
        in_specs=[vmem] * 8,
        out_specs=vmem,
        scratch_shapes=[pltpu.VMEM((2, rows, columns), f32)],
        compiler_params=pltpu.CompilerParams(vmem_limit_bytes=12 * 2**20),
        name="outer",
    )(field, arc_ids, words, inner, layer_1, layer_2, above, below)
    received = lax.all_to_all(parts, "slab", 0, 0, tiled=True)
    merged = pl.pallas_call(
        merge_kernel,
        out_shape=shape((slabs, 4, SUB, LANE), f32),
        in_specs=[vmem],
        out_specs=vmem,
        compiler_params=pltpu.CompilerParams(vmem_limit_bytes=4 * 2**20),
        name="merge",
    )(received)
    pixels = lax.all_to_all(merged, "slab", 0, 0, tiled=True)
    pixels = pixels.reshape(bands, strips, 4, SUB, LANE).transpose(2, 0, 3, 1, 4)
    return pixels.reshape(4, rows, columns)


def solution(mesh):
    in_specs = (P("slab", "tile", None), P("slab", "tile", None), P(), P())
    out_specs = P(None, "tile", None)
    return jax.shard_map(local, mesh=mesh, in_specs=in_specs, out_specs=out_specs, check_vma=False)
```

```python
import functools
import math

import jax
import jax.numpy as jnp
from jax import lax
from jax.experimental import pallas as pl
from jax.experimental.pallas import tpu as pltpu
from jax.sharding import PartitionSpec as P

LOG2E = math.log2(math.e)
SUB = 8
LANE = 128
ALONG_LANES = lax.GatherDimensionNumbers(
    offset_dims=(),
    collapsed_slice_dims=(1,),
    start_index_map=(1,),
    operand_batching_dims=(0,),
    start_indices_batching_dims=(0,),
)
FRACTION = 2.0**30
GREEN_TOP = 2**16 - 1
WIDTH_TOP = 2**10 - 1
FINE = 512.0
CENTRE_UNIT = 2.0**-29
EXTINCTION_SPAN = 2**13


def gathered(table, index):
    return lax.gather(
        table, index[:, :, None], ALONG_LANES, (1, 1), mode=lax.GatherScatterMode.PROMISE_IN_BOUNDS
    )


def whole(value):
    return jnp.floor(value + 0.5).astype(jnp.int32)


def word(high, low, low_span):
    return whole((high - low.astype(jnp.float32)) / low_span) * low_span + low


def fill_tables(arc_tf, tf, raw, arcs, words):
    rows, tf_count = tf.shape
    raw[...] = jnp.zeros_like(raw)
    raw[0:rows, 0:tf_count] = tf[...].astype(jnp.float32)
    arcs[...] = jnp.zeros_like(arcs)
    arcs[0:1, 0 : arc_tf.shape[1]] = arc_tf[...]
    index = jnp.broadcast_to(arcs[0:1, :], (SUB, LANE))
    red, green, blue, extinction, centre, width = [
        gathered(jnp.broadcast_to(raw[j : j + 1, :], (SUB, LANE)), index) for j in range(rows)
    ]
    words[0] = word(red * FRACTION, whole(green * GREEN_TOP), GREEN_TOP + 1)
    words[1] = word(blue * FRACTION, whole(width * FINE), WIDTH_TOP + 1)
    words[2] = word(
        centre / CENTRE_UNIT, EXTINCTION_SPAN - whole(extinction * FINE), EXTINCTION_SPAN
    )


def compose(step_len, vol, arc, words, top, layers, front, back, above, below, totals):
    depth, rows, columns = vol.shape
    strips = columns // LANE
    band = pl.ds(top, SUB)
    lane = lax.broadcasted_iota(jnp.int32, (SUB, LANE), 1)
    row = lax.broadcasted_iota(jnp.int32, (SUB, LANE), 0)
    first_lane, last_lane = lane == 0, lane == LANE - 1
    first_row, last_row = row == 0, row == SUB - 1
    zero = jnp.zeros((SUB, LANE), jnp.float32)
    log_step = math.log2(step_len * LOG2E / FINE)
    totals = list(totals)
    for z in layers:
        center = [vol[z, band, s * LANE : (s + 1) * LANE] for s in range(strips)]
        to_right = [pltpu.roll(c, 1, 1) for c in center]
        to_left = [pltpu.roll(c, LANE - 1, 1) for c in center]
        for s in range(strips):
            cols = slice(s * LANE, (s + 1) * LANE)
            c = center[s]
            index = arc[z, band, cols]
            red_green, blue_width, centre_ext = [gathered(words[j], index) for j in range(3)]
            off = c - centre_ext.astype(jnp.float32) * CENTRE_UNIT
            reach = off * (blue_width & WIDTH_TOP).astype(jnp.float32)
            bell = jnp.exp2(reach * reach * (-LOG2E / FINE**2) + log_step)
            passing = jnp.exp2((centre_ext | -EXTINCTION_SPAN).astype(jnp.float32) * bell)

            left = jnp.where(first_lane, to_right[s - 1] if s else zero, to_right[s])
            right = jnp.where(last_lane, to_left[s + 1] if s + 1 < strips else zero, to_left[s])
            over = above[z, 0:1, cols] if above is not None else vol[z, pl.ds(top - SUB, SUB), cols]
            under = below[z, 0:1, cols] if below is not None else vol[z, pl.ds(top + SUB, SUB), cols]
            up = pltpu.roll(jnp.where(last_row, over, c), 1, 0)
            down = pltpu.roll(jnp.where(first_row, under, c), SUB - 1, 0)
            nearer = vol[z - 1, band, cols] if z else front[0, band, cols]
            farther = vol[z + 1, band, cols] if z + 1 < depth else back[0, band, cols]
            dx = right - left
            dy = down - up
            dz = farther - nearer
            slant = jnp.abs(0.312 * dx + 0.39 * dy + 0.416 * dz)
            shading = 0.35 + slant * lax.rsqrt(4.0 + dx * dx + dy * dy + dz * dz)

            red, green, blue, transmit = totals[s]
            after = transmit * passing
            weight = (transmit - after) * shading
            totals[s] = (
                red + weight * red_green.astype(jnp.float32),
                green + weight * (red_green & GREEN_TOP).astype(jnp.float32),
                blue + weight * blue_width.astype(jnp.float32),
                after,
            )
    return totals


def clear(strips):
    zero = jnp.zeros((SUB, LANE), jnp.float32)
    return [(zero, zero, zero, zero + 1.0)] * strips


def faces_kernel(field, layer_1, layer_2, top, bottom):
    depth, rows, columns = field.shape
    slab_odd = lax.axis_index("slab") % 2
    layer_1[...] = field[pl.ds((1 - slab_odd) * (depth - 1), 1)]
    layer_2[...] = field[pl.ds(slab_odd * (depth - 1), 1)]
    top[...] = field[:, 0:1, :]
    bottom[...] = field[:, rows - 1 :, :]


def inner_kernel(step_len, vol, arc, arc_tf, tf, words, inner, raw, arcs):
    depth, rows, columns = vol.shape
    bands, strips = rows // SUB, columns // LANE
    fill_tables(arc_tf, tf, raw, arcs, words)

    def step(band, carry):
        top = pl.multiple_of(band * SUB, SUB)
        totals = compose(
            step_len, vol, arc, words, top, range(1, depth - 1), None, None, None, None, clear(strips)
        )
        for s in range(strips):
            for j in range(4):
                inner[(band - 1) * strips + s, j] = totals[s][j]
        return carry

    lax.fori_loop(1, bands - 1, step, 0, unroll=3 if (bands - 2) % 3 == 0 else 1)


def outer_kernel(step_len, vol, arc, words, inner, layer_1, layer_2, above, below, parts, halo):
    depth, rows, columns = vol.shape
    bands, strips = rows // SUB, columns // LANE
    slab, tile = lax.axis_index("slab"), lax.axis_index("tile")
    slab_odd = slab % 2
    slab_inner = (slab > 0) & (slab < lax.axis_size("slab") - 1)
    halo[pl.ds(1 - slab_odd, 1)] = layer_1[...]
    halo[pl.ds(slab_odd, 1)] = layer_2[...] * slab_inner.astype(jnp.float32)
    front, back = halo.at[0:1], halo.at[1:2]
    above[...] = above[...] * (tile > 0).astype(jnp.float32)
    below[...] = below[...] * (tile < lax.axis_size("tile") - 1).astype(jnp.float32)
    scale = (1.0 / FRACTION, 1.0 / GREEN_TOP, 1.0 / FRACTION, 1.0)

    def put(band, totals):
        for s in range(strips):
            for j in range(4):
                parts[band * strips + s, j] = totals[s][j] * scale[j]

    def whole_band(band, over, under):
        top = band * SUB
        put(
            band,
            compose(
                step_len, vol, arc, words, top, range(depth), front, back, over, under, clear(strips)
            ),
        )

    def step(band, carry):
        top = pl.multiple_of(band * SUB, SUB)
        at = (step_len, vol, arc, words, top)
        totals = compose(*at, [0], front, back, None, None, clear(strips))
        for s in range(strips):
            red, green, blue, transmit = totals[s]
            behind = [inner[(band - 1) * strips + s, j] for j in range(4)]
            totals[s] = (
                red + transmit * behind[0],
                green + transmit * behind[1],
                blue + transmit * behind[2],
                transmit * behind[3],
            )
        put(band, compose(*at, [depth - 1], front, back, None, None, totals))
        return carry

    lax.fori_loop(1, bands - 1, step, 0, unroll=True)
    whole_band(0, above, None)
    whole_band(bands - 1, None, below)


def merge_kernel(parts, out):
    count = parts.shape[0]
    red, green, blue, transmit = (parts[0, j] for j in range(4))
    for s in range(1, count):
        red = red + transmit * parts[s, 0]
        green = green + transmit * parts[s, 1]
        blue = blue + transmit * parts[s, 2]
        transmit = transmit * parts[s, 3]
    for s in range(count):
        for j, value in enumerate((red, green, blue, 1.0 - transmit)):
            out[s, j] = value


def shifted(value, axis, step):
    count = lax.axis_size(axis)
    if axis == "tile":
        return lax.ppermute(value, axis, [(i, (i + step) % count) for i in range(count)])
    return lax.ppermute(
        value, axis, [(i, i + step) for i in range(count) if 0 <= i + step < count]
    )


def swapped(value, axis, first):
    count = lax.axis_size(axis)
    partner = {i: i for i in range(count)}
    for i in range(first, count - 1, 2):
        partner[i], partner[i + 1] = i + 1, i
    return lax.ppermute(value, axis, list(partner.items()))


def local(field, arc_ids, arc_tf, tf_table):
    depth, rows, columns = field.shape
    slabs = lax.axis_size("slab")
    step_len = 2.0 / (depth * slabs)
    bands, strips = rows // SUB, columns // LANE
    f32 = jnp.float32
    vmem = pl.BlockSpec(memory_space=pltpu.VMEM)
    hbm = pl.BlockSpec(memory_space=pltpu.HBM)
    shape = jax.ShapeDtypeStruct
    layer_1, layer_2, top, bottom = pl.pallas_call(
        faces_kernel,
        out_shape=[shape((1, rows, columns), f32)] * 2 + [shape((depth, 1, columns), f32)] * 2,
        in_specs=[vmem],
        out_specs=[vmem] * 4,
        compiler_params=pltpu.CompilerParams(vmem_limit_bytes=40 * 2**20),
        name="faces",
    )(field)
    layer_2 = swapped(layer_2, "slab", 1)
    layer_1 = swapped(layer_1, "slab", 0)
    above = shifted(bottom, "tile", 1)
    below = shifted(top, "tile", -1)
    words, inner = pl.pallas_call(
        functools.partial(inner_kernel, step_len),
        out_shape=[
            shape((3, SUB, LANE), jnp.int32),
            shape(((bands - 2) * strips, 4, SUB, LANE), f32),
        ],
        in_specs=[vmem] * 4,
        out_specs=[vmem] * 2,
        scratch_shapes=[pltpu.VMEM((SUB, LANE), f32), pltpu.VMEM((SUB, LANE), jnp.int32)],
        compiler_params=pltpu.CompilerParams(vmem_limit_bytes=12 * 2**20),
        cost_estimate=pl.CostEstimate(
            flops=60 * field.size, bytes_accessed=8 * field.size, transcendentals=3 * field.size
        ),
        name="inner",
    )(field, arc_ids, arc_tf[None, :], tf_table)
    parts = pl.pallas_call(
        functools.partial(outer_kernel, step_len),
        out_shape=shape((bands * strips, 4, SUB, LANE), f32),
        in_specs=[vmem] * 8,
        out_specs=vmem,
        scratch_shapes=[pltpu.VMEM((2, rows, columns), f32)],
        compiler_params=pltpu.CompilerParams(vmem_limit_bytes=12 * 2**20),
        name="outer",
    )(field, arc_ids, words, inner, layer_1, layer_2, above, below)
    received = lax.all_to_all(parts, "slab", 0, 0, tiled=True)
    merged = pl.pallas_call(
        merge_kernel,
        out_shape=shape((slabs, 4, SUB, LANE), f32),
        in_specs=[vmem],
        out_specs=vmem,
        compiler_params=pltpu.CompilerParams(vmem_limit_bytes=4 * 2**20),
        name="merge",
    )(received)
    pixels = lax.all_to_all(merged, "slab", 0, 0, tiled=True)
    pixels = pixels.reshape(bands, strips, 4, SUB, LANE).transpose(2, 0, 3, 1, 4)
    return pixels.reshape(4, rows, columns)


def solution(mesh):
    in_specs = (P("slab", "tile", None), P("slab", "tile", None), P(), P())
    out_specs = P(None, "tile", None)
    return jax.shard_map(local, mesh=mesh, in_specs=in_specs, out_specs=out_specs, check_vma=False)
```

```python
import functools
import math

import jax
import jax.numpy as jnp
from jax import lax
from jax.experimental import pallas as pl
from jax.experimental.pallas import tpu as pltpu
from jax.sharding import PartitionSpec as P

LOG2E = math.log2(math.e)
SUB = 8
LANE = 128
ALONG_LANES = lax.GatherDimensionNumbers(
    offset_dims=(),
    collapsed_slice_dims=(1,),
    start_index_map=(1,),
    operand_batching_dims=(0,),
    start_indices_batching_dims=(0,),
)
FRACTION = 2.0**30
GREEN_TOP = 2**16 - 1
WIDTH_TOP = 2**10 - 1
FINE = 512.0
CENTRE_UNIT = 2.0**-29
EXTINCTION_SPAN = 2**13


def gathered(table, index):
    return lax.gather(
        table, index[:, :, None], ALONG_LANES, (1, 1), mode=lax.GatherScatterMode.PROMISE_IN_BOUNDS
    )


def whole(value):
    return jnp.floor(value + 0.5).astype(jnp.int32)


def word(high, low, low_span):
    return whole((high - low.astype(jnp.float32)) / low_span) * low_span + low


def fill_tables(arc_tf, tf, raw, arcs, words):
    rows, tf_count = tf.shape
    raw[...] = jnp.zeros_like(raw)
    raw[0:rows, 0:tf_count] = tf[...].astype(jnp.float32)
    arcs[...] = jnp.zeros_like(arcs)
    arcs[0:1, 0 : arc_tf.shape[1]] = arc_tf[...]
    index = jnp.broadcast_to(arcs[0:1, :], (SUB, LANE))
    red, green, blue, extinction, centre, width = [
        gathered(jnp.broadcast_to(raw[j : j + 1, :], (SUB, LANE)), index) for j in range(rows)
    ]
    words[0] = word(red * FRACTION, whole(green * GREEN_TOP), GREEN_TOP + 1)
    words[1] = word(blue * FRACTION, whole(width * FINE), WIDTH_TOP + 1)
    words[2] = word(
        centre / CENTRE_UNIT, EXTINCTION_SPAN - whole(extinction * FINE), EXTINCTION_SPAN
    )


def compose(step_len, vol, arc, words, top, layers, front, back, above, below, totals):
    depth, rows, columns = vol.shape
    strips = columns // LANE
    band = pl.ds(top, SUB)
    lane = lax.broadcasted_iota(jnp.int32, (SUB, LANE), 1)
    row = lax.broadcasted_iota(jnp.int32, (SUB, LANE), 0)
    first_lane, last_lane = lane == 0, lane == LANE - 1
    first_row, last_row = row == 0, row == SUB - 1
    zero = jnp.zeros((SUB, LANE), jnp.float32)
    log_step = math.log2(step_len * LOG2E / FINE)
    totals = list(totals)
    for z in layers:
        center = [vol[z, band, s * LANE : (s + 1) * LANE] for s in range(strips)]
        to_right = [pltpu.roll(c, 1, 1) for c in center]
        to_left = [pltpu.roll(c, LANE - 1, 1) for c in center]
        for s in range(strips):
            cols = slice(s * LANE, (s + 1) * LANE)
            c = center[s]
            index = arc[z, band, cols]
            red_green, blue_width, centre_ext = [gathered(words[j], index) for j in range(3)]
            off = c - centre_ext.astype(jnp.float32) * CENTRE_UNIT
            reach = off * (blue_width & WIDTH_TOP).astype(jnp.float32)
            bell = jnp.exp2(reach * reach * (-LOG2E / FINE**2) + log_step)
            passing = jnp.exp2((centre_ext | -EXTINCTION_SPAN).astype(jnp.float32) * bell)

            left = jnp.where(first_lane, to_right[s - 1] if s else zero, to_right[s])
            right = jnp.where(last_lane, to_left[s + 1] if s + 1 < strips else zero, to_left[s])
            over = above[z, 0:1, cols] if above is not None else vol[z, pl.ds(top - SUB, SUB), cols]
            under = below[z, 0:1, cols] if below is not None else vol[z, pl.ds(top + SUB, SUB), cols]
            up = pltpu.roll(jnp.where(last_row, over, c), 1, 0)
            down = pltpu.roll(jnp.where(first_row, under, c), SUB - 1, 0)
            nearer = vol[z - 1, band, cols] if z else front[0, band, cols]
            farther = vol[z + 1, band, cols] if z + 1 < depth else back[0, band, cols]
            dx = right - left
            dy = down - up
            dz = farther - nearer
            slant = jnp.abs(0.312 * dx + 0.39 * dy + 0.416 * dz)
            shading = 0.35 + slant * lax.rsqrt(4.0 + dx * dx + dy * dy + dz * dz)

            red, green, blue, transmit = totals[s]
            after = transmit * passing
            weight = (transmit - after) * shading
            totals[s] = (
                red + weight * red_green.astype(jnp.float32),
                green + weight * (red_green & GREEN_TOP).astype(jnp.float32),
                blue + weight * blue_width.astype(jnp.float32),
                after,
            )
    return totals


def clear(strips):
    zero = jnp.zeros((SUB, LANE), jnp.float32)
    return [(zero, zero, zero, zero + 1.0)] * strips


def faces_kernel(field, layer_1, layer_2, top, bottom):
    depth, rows, columns = field.shape
    slab_odd = lax.axis_index("slab") % 2
    layer_1[...] = field[pl.ds((1 - slab_odd) * (depth - 1), 1)]
    layer_2[...] = field[pl.ds(slab_odd * (depth - 1), 1)]
    top[...] = field[:, 0:1, :]
    bottom[...] = field[:, rows - 1 :, :]


def inner_kernel(step_len, vol, arc, arc_tf, tf, words, inner, raw, arcs):
    depth, rows, columns = vol.shape
    bands, strips = rows // SUB, columns // LANE
    fill_tables(arc_tf, tf, raw, arcs, words)

    def step(band, carry):
        top = pl.multiple_of(band * SUB, SUB)
        totals = compose(
            step_len, vol, arc, words, top, range(1, depth - 1), None, None, None, None, clear(strips)
        )
        for s in range(strips):
            for j in range(4):
                inner[(band - 1) * strips + s, j] = totals[s][j]
        return carry

    lax.fori_loop(1, bands - 1, step, 0, unroll=3 if (bands - 2) % 3 == 0 else 1)


def outer_kernel(step_len, vol, arc, words, inner, layer_1, layer_2, above, below, parts, halo):
    depth, rows, columns = vol.shape
    bands, strips = rows // SUB, columns // LANE
    slab, tile = lax.axis_index("slab"), lax.axis_index("tile")
    slab_odd = slab % 2
    slab_inner = (slab > 0) & (slab < lax.axis_size("slab") - 1)
    halo[pl.ds(1 - slab_odd, 1)] = layer_1[...]
    halo[pl.ds(slab_odd, 1)] = layer_2[...] * slab_inner.astype(jnp.float32)
    front, back = halo.at[0:1], halo.at[1:2]
    above[...] = above[...] * (tile > 0).astype(jnp.float32)
    below[...] = below[...] * (tile < lax.axis_size("tile") - 1).astype(jnp.float32)
    scale = (1.0 / FRACTION, 1.0 / GREEN_TOP, 1.0 / FRACTION, 1.0)

    def put(band, totals):
        for s in range(strips):
            for j in range(4):
                parts[band * strips + s, j] = totals[s][j] * scale[j]

    def whole_band(band, over, under):
        top = band * SUB
        put(
            band,
            compose(
                step_len, vol, arc, words, top, range(depth), front, back, over, under, clear(strips)
            ),
        )

    def step(band, carry):
        top = pl.multiple_of(band * SUB, SUB)
        at = (step_len, vol, arc, words, top)
        totals = compose(*at, [0], front, back, None, None, clear(strips))
        for s in range(strips):
            red, green, blue, transmit = totals[s]
            behind = [inner[(band - 1) * strips + s, j] for j in range(4)]
            totals[s] = (
                red + transmit * behind[0],
                green + transmit * behind[1],
                blue + transmit * behind[2],
                transmit * behind[3],
            )
        put(band, compose(*at, [depth - 1], front, back, None, None, totals))
        return carry

    lax.fori_loop(1, bands - 1, step, 0, unroll=True)
    whole_band(0, above, None)
    whole_band(bands - 1, None, below)


def merge_kernel(order, parts, out):
    count = parts.shape[0]
    nearest, *others = [order.index(slab) for slab in range(count)]
    red, green, blue, transmit = (parts[nearest, j] for j in range(4))
    for s in others:
        red = red + transmit * parts[s, 0]
        green = green + transmit * parts[s, 1]
        blue = blue + transmit * parts[s, 2]
        transmit = transmit * parts[s, 3]
    for s in range(count):
        for j, value in enumerate((red, green, blue, 1.0 - transmit)):
            out[s, j] = value


def shifted(value, axis, step):
    count = lax.axis_size(axis)
    if axis == "tile":
        return lax.ppermute(value, axis, [(i, (i + step) % count) for i in range(count)])
    return lax.ppermute(
        value, axis, [(i, i + step) for i in range(count) if 0 <= i + step < count]
    )


def swapped(value, axis, first):
    count = lax.axis_size(axis)
    partner = {i: i for i in range(count)}
    for i in range(first, count - 1, 2):
        partner[i], partner[i + 1] = i + 1, i
    return lax.ppermute(value, axis, list(partner.items()))


def local(field, arc_ids, arc_tf, tf_table):
    depth, rows, columns = field.shape
    slabs = lax.axis_size("slab")
    step_len = 2.0 / (depth * slabs)
    bands, strips = rows // SUB, columns // LANE
    f32 = jnp.float32
    vmem = pl.BlockSpec(memory_space=pltpu.VMEM)
    hbm = pl.BlockSpec(memory_space=pltpu.HBM)
    shape = jax.ShapeDtypeStruct
    layer_1, layer_2, top, bottom = pl.pallas_call(
        faces_kernel,
        out_shape=[shape((1, rows, columns), f32)] * 2 + [shape((depth, 1, columns), f32)] * 2,
        in_specs=[vmem],
        out_specs=[vmem] * 4,
        compiler_params=pltpu.CompilerParams(vmem_limit_bytes=40 * 2**20),
        name="faces",
    )(field)
    layer_2 = swapped(layer_2, "slab", 1)
    layer_1 = swapped(layer_1, "slab", 0)
    above = shifted(bottom, "tile", 1)
    below = shifted(top, "tile", -1)
    words, inner = pl.pallas_call(
        functools.partial(inner_kernel, step_len),
        out_shape=[
            shape((3, SUB, LANE), jnp.int32),
            shape(((bands - 2) * strips, 4, SUB, LANE), f32),
        ],
        in_specs=[vmem] * 4,
        out_specs=[vmem] * 2,
        scratch_shapes=[pltpu.VMEM((SUB, LANE), f32), pltpu.VMEM((SUB, LANE), jnp.int32)],
        compiler_params=pltpu.CompilerParams(vmem_limit_bytes=12 * 2**20),
        cost_estimate=pl.CostEstimate(
            flops=60 * field.size, bytes_accessed=8 * field.size, transcendentals=3 * field.size
        ),
        name="inner",
    )(field, arc_ids, arc_tf[None, :], tf_table)
    parts = pl.pallas_call(
        functools.partial(outer_kernel, step_len),
        out_shape=shape((bands * strips, 4, SUB, LANE), f32),
        in_specs=[vmem] * 8,
        out_specs=vmem,
        scratch_shapes=[pltpu.VMEM((2, rows, columns), f32)],
        compiler_params=pltpu.CompilerParams(vmem_limit_bytes=12 * 2**20),
        name="outer",
    )(field, arc_ids, words, inner, layer_1, layer_2, above, below)
    order = list(range(slabs - 1, -1, -1))
    received = lax.all_to_all(parts, "slab", 0, 0, axis_index_groups=[order], tiled=True)
    merged = pl.pallas_call(
        functools.partial(merge_kernel, order),
        out_shape=shape((slabs, 4, SUB, LANE), f32),
        in_specs=[vmem],
        out_specs=vmem,
        compiler_params=pltpu.CompilerParams(vmem_limit_bytes=4 * 2**20),
        name="merge",
    )(received)
    pixels = lax.all_to_all(merged, "slab", 0, 0, axis_index_groups=[order], tiled=True)
    pixels = pixels.reshape(bands, strips, 4, SUB, LANE).transpose(2, 0, 3, 1, 4)
    return pixels.reshape(4, rows, columns)


def solution(mesh):
    in_specs = (P("slab", "tile", None), P("slab", "tile", None), P(), P())
    out_specs = P(None, "tile", None)
    return jax.shard_map(local, mesh=mesh, in_specs=in_specs, out_specs=out_specs, check_vma=False)
```
